1024 devices in a mesh: pipe: 4 (over x), expert: 64 (over y_hi, z, core), dp: 4 (over y_lo).
Axes of the slice: x: 4, y: 8 (y_hi: 2, y_lo: 4; y = y_hi * 4 + y_lo), z: 16, core: 2. Of those that a mesh axis runs over, the one named last changes fastest.
Arguments:
- x_fwd: bfloat16 [4, 2048, 3584], P('pipe', ('expert', 'dp')), may hold values from -6 to 6
- ids_fwd: int32 [4, 2048, 2], P('pipe', ('expert', 'dp')), may hold values from 0 to 15, all different within a row; in each aligned block of 8 rows (0 to 7, 8 to 15, ..., all dimensions but the last counted through in order) at most 2 rows name the same one
- prob_fwd: float32 [4, 2048, 2], P('pipe', ('expert', 'dp')), may hold values from 0.2 to 1
- grad_bwd: bfloat16 [4, 2048, 3584], P('pipe', ('expert', 'dp')), may hold values from -1.796875 to 1.796875
- ids_bwd: int32 [4, 2048, 2], P('pipe', ('expert', 'dp')), may hold values from 0 to 15, all different within a row; in each aligned block of 8 rows (0 to 7, 8 to 15, ..., all dimensions but the last counted through in order) at most 2 rows name the same one
- prob_bwd: float32 [4, 2048, 2], P('pipe', ('expert', 'dp')), may hold values from 0.2 to 1
- pre_bwd: bfloat16 [4, 2048, 2, 2, 1024], P('pipe', ('expert', 'dp')), may hold values from -6 to 6
- w_gate: bfloat16 [4, 3584, 16384], P('pipe', None, 'expert'), may hold values from -0.09375 to 0.09375
- w_up: bfloat16 [4, 3584, 16384], P('pipe', None, 'expert'), may hold values from -0.09375 to 0.09375
- w_down: bfloat16 [4, 16384, 3584], P('pipe', 'expert'), may hold values from -0.375 to 0.375
Outputs:
- next_input: bfloat16 [4, 2048, 3584], P('pipe', ('expert', 'dp'))
- grad_input: bfloat16 [4, 2048, 3584], P('pipe', ('expert', 'dp'))
- grad_down: float32 [4, 16384, 3584], P('pipe', ('expert', 'dp'))
The draws below stay inside these ranges and needn't reach their ends.
Inputs may be any that keep to these rules, and one draw needn't show every extreme that they name: `ids_fwd`: in each aligned block of 8 rows (the tokens of one device) no expert is named by more than 2 rows, a bound that some block reaches. `ids_bwd`: same bound per aligned block of 8 rows as for the forward routes.
All inputs are finite; a program needn't handle non-finite values.
Results may differ from the reference program's by a relative error of at most 0.011.
Values may be sent and summed in bfloat16 or wider, within the bound.
No kernel may reach another device: no remote copies, remote signals or barrier semaphores. Data moves between devices by JAX's collectives and lax.ppermute only.
A program may use at most 32 MiB of HBM per device.

```python
import math
import jax
import jax.numpy as jnp
import numpy as np
from jax import lax

D = 3584
TOK_DEV = 8
H_DEV = 256
SHARDS = 4
EXPERTS = 16
HID = 1024
TOPK = 2
CAP = 2
TOKENS = 2048
N_PIPE = 4
N_EXPERT = 64
N_DP = 4


def level_of(own_key, dims, shards, low, high):
    loudness, own = 1.0, jax.random.fold_in(own_key, 6)
    for position, blocks in shards:
        draws = jnp.exp(jax.random.uniform(jax.random.fold_in(own, position), (blocks,), jnp.float32, low / len(shards), high / len(shards)))
        loudness = loudness * jnp.repeat(draws, dims[position] // blocks).reshape([-1 if axis == position else 1 for axis in range(len(dims))])
    return loudness


def routed_block(own_key, own, number, rows, count, top, bound, lean):
    ranking = jax.random.permutation(own_key, count)
    packed, common = portions_of(count, rows * top, bound, lean, True), portions_of(count, rows * top, bound, lean, False)
    places = jnp.arange(count)

    def named(tallies, rotation):
        used = int((tallies > 0).sum())
        fixed = max(1, used // 4)
        shifted = fixed + (places - fixed + rotation * (used - fixed)) % max(1, count - fixed)
        return jnp.zeros((count,), jnp.int32).at[ranking[jnp.where(places < fixed, places, shifted)]].set(jnp.asarray(tallies, jnp.int32))

    tallies = jnp.where(number % 4 == 0, named(packed, number // 4), named(common, number - number // 4 - 1))
    mixed = jax.random.permutation(jax.random.fold_in(own, 3), count)
    giver, receiver = mixed[0:count // 2 * 2:2], mixed[1:count // 2 * 2:2]
    room = jnp.minimum(tallies[giver] - 1, bound - tallies[receiver]) // 2
    room = jnp.where((giver == ranking[0]) | (receiver == ranking[0]) | (tallies[receiver] == 0), 0, jnp.maximum(room, 0))
    shifted = jax.random.randint(jax.random.fold_in(own, 4), (count // 2,), 0, 1 << 20) % (room + 1)
    tallies = tallies.at[giver].add(-shifted).at[receiver].add(shifted)
    items = jnp.searchsorted(jnp.cumsum(tallies), jnp.arange(rows * top), side="right").astype(jnp.int32)
    listing = items.reshape(top, rows).T
    listing = listing[jax.random.permutation(jax.random.fold_in(own, 1), rows)]
    rotation = jax.random.randint(jax.random.fold_in(own, 2), (rows, 1), 0, top)
    return jnp.take_along_axis(listing, (jnp.arange(top)[None, :] + rotation) % top, axis=1)


def portions_of(amount, total, limit, skew, full):
    weights = [(1 << 20) // math.isqrt(rank ** skew) + 1 for rank in range(1, amount + 1)]
    largest = limit if full else min(limit, max(-(-total // amount), total * weights[0] // sum(weights)))
    least = 1 if total - largest >= amount - 1 else 0
    given, surplus = [largest] + [least] * (amount - 1), total - largest - least * (amount - 1)
    while surplus > 0:
        candidates = [i for i in range(1, amount) if given[i] < largest] or [i for i in range(1, amount) if given[i] < limit]
        mass, budget = sum([weights[i] for i in candidates]), surplus
        for i in candidates:
            extra = min(limit - given[i], max(1, budget * weights[i] // mass), surplus)
            given[i] = given[i] + extra
            surplus = surplus - extra
    return np.array(given)


def bell_draw(own_key, shape, spread, reach, pieces=(), kind=jnp.bfloat16):
    entries = jax.random.normal(own_key, shape, jnp.float32) * spread
    if len(pieces) > 0:
        entries = level_of(own_key, shape, pieces, -0.22, 0.18) * entries
    return jnp.clip(entries, min=-reach, max=reach).astype(kind)


def setup_inputs(seed: int = 0) -> dict:
    key_list = jax.random.split(jax.random.key(seed), 11)
    x_fwd = bell_draw(key_list[0], (N_PIPE, TOKENS, D), 1.0, 6.0, ((0, 4), (1, 256)))
    ids_fwd_keys = jax.random.split(jax.random.fold_in(key_list[1], 1), N_PIPE * TOKENS // TOK_DEV)
    ids_fwd_turns = jax.random.permutation(jax.random.fold_in(key_list[1], 3), N_PIPE * TOKENS // TOK_DEV)
    ids_fwd = jax.vmap(lambda own, number: routed_block(jax.random.fold_in(key_list[1], 2), own, number, TOK_DEV, EXPERTS, TOPK, CAP, 2))(ids_fwd_keys, ids_fwd_turns).reshape((N_PIPE, TOKENS, TOPK))
    prob_fwd = jnp.clip(0.2 + 0.8 * jax.random.uniform(key_list[2], (N_PIPE, TOKENS, TOPK), jnp.float32) ** level_of(key_list[2], (N_PIPE, TOKENS, TOPK), ((0, 4), (1, 256)), -0.2, 0.2), 0.2, 1.0)
    grad_bwd = bell_draw(key_list[3], (N_PIPE, TOKENS, D), 0.3, 1.796875, ((0, 4), (1, 256)))
    ids_bwd_keys = jax.random.split(jax.random.fold_in(key_list[4], 1), N_PIPE * TOKENS // TOK_DEV)
    ids_bwd_turns = jax.random.permutation(jax.random.fold_in(key_list[4], 3), N_PIPE * TOKENS // TOK_DEV)
    ids_bwd = jax.vmap(lambda own, number: routed_block(jax.random.fold_in(key_list[4], 2), own, number, TOK_DEV, EXPERTS, TOPK, CAP, 2))(ids_bwd_keys, ids_bwd_turns).reshape((N_PIPE, TOKENS, TOPK))
    prob_bwd = jnp.clip(0.2 + 0.8 * jax.random.uniform(key_list[5], (N_PIPE, TOKENS, TOPK), jnp.float32) ** level_of(key_list[5], (N_PIPE, TOKENS, TOPK), ((0, 4), (1, 256)), -0.2, 0.2), 0.2, 1.0)
    pre_bwd = bell_draw(key_list[6], (N_PIPE, TOKENS, TOPK, 2, HID), 1.0, 6.0, ((0, 4), (1, 256)))
    w_gate = bell_draw(key_list[7], (N_PIPE, D, EXPERTS * HID), D ** -0.5, 0.09375, ((0, 4), (2, 64)))
    w_up = bell_draw(key_list[8], (N_PIPE, D, EXPERTS * HID), D ** -0.5, 0.09375, ((0, 4), (2, 64)))
    w_down = bell_draw(key_list[9], (N_PIPE, EXPERTS * HID, D), H_DEV ** -0.5, 0.375, ((0, 4), (1, 64)))
    return {"x_fwd": x_fwd, "ids_fwd": ids_fwd, "prob_fwd": prob_fwd, "grad_bwd": grad_bwd, "ids_bwd": ids_bwd, "prob_bwd": prob_bwd, "pre_bwd": pre_bwd, "w_gate": w_gate, "w_up": w_up, "w_down": w_down}


def silu_pair(value):
    sig = jax.nn.sigmoid(value)
    return value * sig, sig * (1.0 + value * (1.0 - sig))


def to_bf(value):
    return lax.optimization_barrier(value.astype(jnp.bfloat16)).astype(jnp.float32)


def section_pass(x_in, id_f, p_f, g_in, id_b, p_b, pre_in, w_g, w_u, w_d):
    high = lax.Precision.HIGHEST
    labels = jnp.arange(EXPERTS, dtype=jnp.int32)
    pick_f = (id_f[:, :, None] == labels[None, None, :]).astype(jnp.float32)
    coef_f = jnp.sum(pick_f * p_f[:, :, None], axis=1)
    pick_b = (id_b[:, :, None] == labels[None, None, :]).astype(jnp.float32)
    coef_b = jnp.sum(pick_b * p_b[:, :, None], axis=1)
    x_all = x_in.astype(jnp.float32)
    dy_all = g_in.astype(jnp.float32)
    pre_all = pre_in.astype(jnp.float32)
    count = x_in.shape[0]

    def per_expert(carry, expert):
        out_acc, dx_acc = carry
        start = (expert * HID).astype(jnp.int32)
        wg_e = lax.dynamic_slice_in_dim(w_g, start, HID, 1).astype(jnp.float32)
        wu_e = lax.dynamic_slice_in_dim(w_u, start, HID, 1).astype(jnp.float32)
        wd_e = lax.dynamic_slice_in_dim(w_d, start, HID, 0).astype(jnp.float32)
        gate_pre = jnp.dot(x_all, wg_e, precision=high)
        up_pre = jnp.dot(x_all, wu_e, precision=high)
        act, _ = silu_pair(gate_pre)
        hidden = to_bf(act * up_pre).reshape(count, SHARDS, H_DEV)
        wd_blocks = wd_e.reshape(SHARDS, H_DEV, D)
        part = to_bf(jnp.einsum('tsh,shd->tsd', hidden, wd_blocks, precision=high))
        weight_f = jnp.take(coef_f, expert, axis=1)
        out_acc = out_acc + weight_f[:, None] * jnp.sum(part, axis=1)

        weight_b = jnp.take(coef_b, expert, axis=1)
        grad_rows = to_bf(weight_b[:, None] * dy_all)
        chosen = jnp.take(pick_b, expert, axis=2)
        pre_e = jnp.sum(chosen[:, :, None, None] * pre_all, axis=1)
        act_b, slope = silu_pair(pre_e[:, 0])
        up_b = pre_e[:, 1]
        hidden_b = to_bf(act_b * up_b)
        dhid = jnp.dot(grad_rows, wd_e.T, precision=high)
        d_gate = to_bf(dhid * up_b * slope).reshape(count, SHARDS, H_DEV)
        d_up = to_bf(dhid * act_b).reshape(count, SHARDS, H_DEV)
        wg_blocks = wg_e.reshape(D, SHARDS, H_DEV)
        wu_blocks = wu_e.reshape(D, SHARDS, H_DEV)
        dx_part = to_bf(jnp.einsum('tsh,dsh->tsd', d_gate, wg_blocks, precision=high)
                        + jnp.einsum('tsh,dsh->tsd', d_up, wu_blocks, precision=high))
        dx_acc = dx_acc + jnp.sum(dx_part, axis=1)

        h_rep = hidden_b.reshape(N_EXPERT, N_DP, TOK_DEV, HID)
        g_rep = grad_rows.reshape(N_EXPERT, N_DP, TOK_DEV, D)
        per_rep = to_bf(jnp.einsum('jrth,jrtd->rhd', h_rep, g_rep, precision=high))
        return (out_acc, dx_acc), jnp.sum(per_rep, axis=0)

    zero = jnp.zeros((count, D), jnp.float32)
    (out_acc, dx_acc), grads = lax.scan(per_expert, (zero, zero), jnp.arange(EXPERTS, dtype=jnp.int32))
    return out_acc.astype(jnp.bfloat16), dx_acc.astype(jnp.bfloat16), grads.reshape(EXPERTS * HID, D)


def reference(x_fwd, ids_fwd, prob_fwd, grad_bwd, ids_bwd, prob_bwd, pre_bwd, w_gate, w_up, w_down):
    routed_all = []
    dx_all = []
    grad_all = []
    for section in range(N_PIPE):
        routed, dx_section, grad_section = section_pass(x_fwd[section], ids_fwd[section], prob_fwd[section], grad_bwd[section],
                                                  ids_bwd[section], prob_bwd[section], pre_bwd[section],
                                                  w_gate[section], w_up[section], w_down[section])
        routed_all.append(routed)
        dx_all.append(dx_section)
        grad_all.append(grad_section)
    next_input = jnp.roll(jnp.stack(routed_all), 1, axis=0)
    return next_input, jnp.stack(dx_all), jnp.stack(grad_all)
```

```python
import functools

import jax
import jax.numpy as jnp
from jax import lax
from jax.experimental import pallas as pl
from jax.experimental.pallas import tpu as pltpu
from jax.sharding import PartitionSpec as P

EXPERTS = 16
SLOTS = 2
SHARDS = 4
ROWS = EXPERTS * SLOTS
BF = jnp.bfloat16
F32 = jnp.float32


def route_groups(replicas):
    groups = []
    for r in range(replicas):
        for shard in range(SHARDS):
            groups.append(
                [
                    (e * SHARDS + shard) * replicas
                    + (r if e < EXPERTS // 2 else replicas - 1 - r)
                    for e in range(EXPERTS)
                ]
            )
    return groups


def route(rows):
    groups = route_groups(lax.axis_size("dp"))
    return lax.all_to_all(
        rows,
        ("expert", "dp"),
        split_axis=0,
        concat_axis=0,
        tiled=True,
        axis_index_groups=groups,
    )


def swap(rows, bit):
    count = lax.axis_size("expert")
    return lax.ppermute(rows, "expert", [(i, i ^ bit) for i in range(count)])


def selections(ids_ref):
    tokens, chosen = ids_ref.shape
    lane = lax.broadcasted_iota(jnp.int32, (tokens, ROWS), 1)
    hits = [ids_ref[:, k : k + 1] == lane // SLOTS for k in range(chosen)]
    hit = jnp.where(functools.reduce(jnp.logical_or, hits), 1.0, 0.0)
    row = lax.broadcasted_iota(jnp.int32, (tokens, tokens), 0)
    col = lax.broadcasted_iota(jnp.int32, (tokens, tokens), 1)
    earlier = jnp.where(col < row, 1.0, 0.0)
    before = jnp.dot(earlier, hit, preferred_element_type=F32)
    slot = (lane % SLOTS).astype(F32)
    return [jnp.where(jnp.logical_and(h, before == slot), 1.0, 0.0) for h in hits]


def pick(sel, rows):
    return lax.dot_general(
        sel.astype(BF), rows, (((0,), (0,)), ((), ())), preferred_element_type=F32
    )


def build_kernel(
    shard_ref, ids_f, prob_f, x_ref, ids_b, prob_b, g_ref, pre_ref,
    sx_ref, sg_ref, wf_ref, tb_ref,
):
    sel_b = selections(ids_b)
    width = g_ref.shape[1]
    total = jnp.zeros((ROWS, width), F32)
    grad = g_ref[...].astype(F32)
    for k, sel in enumerate(sel_b):
        total += pick(sel, (prob_b[:, k : k + 1] * grad).astype(BF))
    sg_ref[:, :width] = total.astype(BF)
    chosen = len(sel_b)
    hid = pre_ref.shape[1] // (2 * chosen)
    units = hid // SHARDS
    shard = shard_ref[0]
    for step in range(SHARDS):
        for half in range(2):
            part = jnp.zeros((ROWS, units), F32)
            for k, sel in enumerate(sel_b):
                start = (2 * k + half) * hid + (shard ^ step) * units
                start = pl.multiple_of(start, 128)
                part += pick(sel, pre_ref[:, pl.ds(start, units)])
            at = width + (2 * step + half) * units
            sg_ref[:, at : at + units] = part.astype(BF)
    tb_ref[...] = sel_b[0] + sel_b[1]
    sel_f = selections(ids_f)
    sx_ref[...] = pick(sel_f[0] + sel_f[1], x_ref[...]).astype(BF)
    wf_ref[...] = sel_f[0] * prob_f[:, 0:1] + sel_f[1] * prob_f[:, 1:2]


def build_rows(shard, ids_f, prob_f, x, ids_b, prob_b, grad, pre):
    tokens, width = x.shape
    pre_width = pre.shape[1] // 2
    vmem = pl.BlockSpec(memory_space=pltpu.VMEM)
    return pl.pallas_call(
        build_kernel,
        out_shape=(
            jax.ShapeDtypeStruct((ROWS, width), BF),
            jax.ShapeDtypeStruct((ROWS, width + pre_width), BF),
            jax.ShapeDtypeStruct((tokens, ROWS), F32),
            jax.ShapeDtypeStruct((tokens, ROWS), F32),
        ),
        in_specs=[pl.BlockSpec(memory_space=pltpu.SMEM)] + [vmem] * 7,
        out_specs=(vmem,) * 4,
        cost_estimate=pl.CostEstimate(
            flops=4 * ROWS * tokens * width, bytes_accessed=2 << 20, transcendentals=0
        ),
        compiler_params=pltpu.CompilerParams(vmem_limit_bytes=16 << 20),
        name="build_rows",
    )(shard, ids_f, prob_f, x, ids_b, prob_b, grad, pre)


def silu_pair(value):
    sig = jax.nn.sigmoid(value)
    return (value * sig, sig * (1.0 + value * (1.0 - sig)))


CONTRACT = (((1,), (1,)), ((), ()))


def reduce_shards(partial):
    quarter = partial.shape[0] // SHARDS
    got = swap(partial[2 * quarter :].astype(BF), 1)
    pair = partial[: 2 * quarter] + got.astype(F32)
    got = swap(pair[quarter:].astype(BF), 2)
    return (pair[:quarter] + got.astype(F32)).astype(BF)


def routed_back(rows):
    width = rows.shape[1]
    back = route(rows.reshape(EXPERTS, SLOTS, width))
    return back.reshape(ROWS, width)


def combine(table, rows):
    return lax.dot_general(
        table,
        rows.astype(F32),
        (((1,), (0,)), ((), ())),
        precision=lax.Precision.HIGHEST,
        preferred_element_type=F32,
    ).astype(BF)


def on_device(x_fwd, ids_fwd, prob_fwd, grad_bwd, ids_bwd, prob_bwd, pre_bwd, w_gate, w_up, w_down):
    tokens, width = x_fwd.shape[1:]
    wg, wu, wd = w_gate[0], w_up[0], w_down[0]
    units = wg.shape[1]
    shard = (lax.axis_index("expert") % SHARDS).astype(jnp.int32).reshape(1)
    send_x, send_g, table_f, table_b = build_rows(
        shard, ids_fwd[0], prob_fwd[0], x_fwd[0], ids_bwd[0], prob_bwd[0], grad_bwd[0],
        pre_bwd[0].reshape(tokens, -1),
    )

    got_g = route(send_g.reshape(EXPERTS, SLOTS, -1)).reshape(ROWS, -1)
    got_x = route(send_x.reshape(EXPERTS, SLOTS, -1)).reshape(ROWS, -1)

    near, far = width + 2 * units, width + 4 * units
    other = swap(jnp.concatenate([got_g[:, :width], got_g[:, far:]], axis=1), 2)
    mine = jnp.concatenate([got_g[:, :far], other], axis=0)
    beside = swap(jnp.concatenate([mine[:, :width], mine[:, near:]], axis=1), 1)
    rows = jnp.concatenate([mine[:, :near], beside], axis=0)
    flat_g = rows[:, :width]
    pre = rows[:, width:].astype(F32)
    gate_pre, up_pre = pre[:, :units], pre[:, units:]
    act, slope = silu_pair(gate_pre)
    hidden = (act * up_pre).astype(BF)
    grad_rows = lax.psum_scatter(
        lax.dot_general(
            hidden, flat_g, (((0,), (0,)), ((), ())), preferred_element_type=F32
        ).astype(BF),
        "dp",
        scatter_dimension=0,
        tiled=True,
    ).astype(F32)
    dhid = lax.dot_general(flat_g, wd, CONTRACT, preferred_element_type=F32)
    d_gate = (dhid * up_pre * slope).astype(BF)
    d_up = (dhid * act).astype(BF)
    dx_part = lax.dot_general(d_gate, wg, CONTRACT, preferred_element_type=F32)
    dx_part = dx_part + lax.dot_general(d_up, wu, CONTRACT, preferred_element_type=F32)
    back_dx = routed_back(reduce_shards(dx_part))

    mine = jnp.concatenate([got_x, swap(got_x, 2)], axis=0)
    rows = jnp.concatenate([mine, swap(mine, 1)], axis=0)
    act, _ = silu_pair(jnp.dot(rows, wg, preferred_element_type=F32))
    up = jnp.dot(rows, wu, preferred_element_type=F32)
    y_part = jnp.dot((act * up).astype(BF), wd, preferred_element_type=F32)
    back_y = routed_back(reduce_shards(y_part))

    routed = combine(table_f, back_y)
    sections = lax.axis_size("pipe")
    moved = lax.ppermute(routed, "pipe", [(i, (i + 1) % sections) for i in range(sections)])
    grad_input = combine(table_b, back_dx)
    return (moved[None], grad_input[None], grad_rows[None])


def solution(mesh):
    token = P("pipe", ("expert", "dp"), None)
    in_specs = (
        token, token, token, token, token, token,
        P("pipe", ("expert", "dp"), None, None, None),
        P("pipe", None, "expert"),
        P("pipe", None, "expert"),
        P("pipe", "expert", None),
    )
    return jax.shard_map(
        on_device, mesh=mesh, in_specs=in_specs, out_specs=(token, token, token), check_vma=False
    )
```

```python
import functools

import jax
import jax.numpy as jnp
from jax import lax
from jax.experimental import pallas as pl
from jax.experimental.pallas import tpu as pltpu
from jax.sharding import PartitionSpec as P

EXPERTS = 16
SLOTS = 2
SHARDS = 4
ROWS = EXPERTS * SLOTS
BF = jnp.bfloat16
F32 = jnp.float32


def route_groups(replicas):
    groups = []
    for r in range(replicas):
        for shard in range(SHARDS):
            groups.append(
                [
                    (e * SHARDS + (shard ^ 2 * far_half(e))) * replicas
                    + (r if e < EXPERTS // 2 else replicas - 1 - r)
                    for e in range(EXPERTS)
                ]
            )
    return groups


def far_half(expert):
    ring = EXPERTS // 2
    return expert % ring // (ring // 2)


def route(rows):
    groups = route_groups(lax.axis_size("dp"))
    return lax.all_to_all(
        rows,
        ("expert", "dp"),
        split_axis=0,
        concat_axis=0,
        tiled=True,
        axis_index_groups=groups,
    )


def swap(rows, bit):
    count = lax.axis_size("expert")
    return lax.ppermute(rows, "expert", [(i, i ^ bit) for i in range(count)])


def selections(ids_ref):
    chosen, tokens = ids_ref.shape
    row = lax.broadcasted_iota(jnp.int32, (ROWS, tokens), 0)
    hits = [ids_ref[k : k + 1, :] == row // SLOTS for k in range(chosen)]
    hit = jnp.where(functools.reduce(jnp.logical_or, hits), 1.0, 0.0)
    first = lax.broadcasted_iota(jnp.int32, (tokens, tokens), 0)
    second = lax.broadcasted_iota(jnp.int32, (tokens, tokens), 1)
    earlier = jnp.where(first < second, 1.0, 0.0)
    before = jnp.dot(hit, earlier, preferred_element_type=F32)
    slot = (row % SLOTS).astype(F32)
    return [jnp.where(jnp.logical_and(h, before == slot), 1.0, 0.0) for h in hits]


def pick(sel, rows):
    return jnp.dot(sel.astype(BF), rows, preferred_element_type=F32)


def build_kernel(shard_ref, *refs):
    hbm, (send_ref, wf_ref, tb_ref), held, sem = refs[:7], refs[7:10], refs[10:17], refs[17]
    copies = [
        pltpu.make_async_copy(src, dst, sem.at[i]) for i, (src, dst) in enumerate(zip(hbm, held))
    ]
    for copy in copies:
        copy.start()
    for copy in copies:
        copy.wait()
    ids_f, prob_f, x_ref, ids_b, prob_b, g_ref, pre_ref = held
    width = g_ref.shape[1]
    sel_b = selections(ids_b)
    both = functools.reduce(jnp.add, sel_b)
    scaled = functools.reduce(jnp.add, [s * prob_b[k : k + 1, :] for k, s in enumerate(sel_b)])
    scale = jnp.sum(scaled, axis=1, keepdims=True)
    send_ref[:, :width] = (scale * pick(both, g_ref[...])).astype(BF)
    chosen = len(sel_b)
    hid = pre_ref.shape[1] // (2 * chosen)
    units = hid // SHARDS
    shard = shard_ref[0]
    blocks = []
    for step in range(SHARDS):
        halves = []
        for half in range(2):
            part = jnp.zeros((ROWS, units), F32)
            for k, sel in enumerate(sel_b):
                start = (2 * k + half) * hid + (shard ^ step) * units
                start = pl.multiple_of(start, 128)
                part += pick(sel, pre_ref[:, pl.ds(start, units)])
            halves.append(part)
        blocks.append(halves)
    expert = lax.broadcasted_iota(jnp.int32, (ROWS, units), 0) // SLOTS
    crosses = far_half(expert) != shard_ref[1]
    for step in range(SHARDS):
        for half in range(2):
            at = width + (2 * step + half) * units
            part = jnp.where(crosses, blocks[step ^ 2][half], blocks[step][half])
            send_ref[:, at : at + units] = part.astype(BF)
    tb_ref[...] = both
    sel_f = selections(ids_f)
    send_ref[:, width + 2 * hid :] = pick(functools.reduce(jnp.add, sel_f), x_ref[...]).astype(BF)
    wf_ref[...] = functools.reduce(
        jnp.add, [s * prob_f[k : k + 1, :] for k, s in enumerate(sel_f)]
    )


VMEM = pl.BlockSpec(memory_space=pltpu.VMEM)


def build_rows(place, *arrays):
    x, pre = arrays[2], arrays[6]
    tokens, width = x.shape
    total = 2 * width + pre.shape[1] // 2
    return pl.pallas_call(
        build_kernel,
        out_shape=(
            jax.ShapeDtypeStruct((ROWS, total), BF),
            jax.ShapeDtypeStruct((ROWS, tokens), F32),
            jax.ShapeDtypeStruct((ROWS, tokens), F32),
        ),
        in_specs=[pl.BlockSpec(memory_space=pltpu.SMEM)]
        + [pl.BlockSpec(memory_space=pl.ANY)] * len(arrays),
        out_specs=(VMEM,) * 3,
        scratch_shapes=[pltpu.VMEM(a.shape, a.dtype) for a in arrays]
        + [pltpu.SemaphoreType.DMA((len(arrays),))],
        cost_estimate=pl.CostEstimate(
            flops=4 * ROWS * tokens * width, bytes_accessed=2 << 20, transcendentals=0
        ),
        compiler_params=pltpu.CompilerParams(vmem_limit_bytes=48 << 20),
        name="build_rows",
    )(place, *arrays)


def silu_pair(value):
    sig = jax.nn.sigmoid(value)
    return (value * sig, sig * (1.0 + value * (1.0 - sig)))


CONTRACT = (((1,), (1,)), ((), ()))
CHUNK = 512


def call(kernel, outs, flops, *arrays):
    moved = sum(a.size * a.dtype.itemsize for a in arrays)
    moved += sum(o.size * o.dtype.itemsize for o in outs)
    return pl.pallas_call(
        kernel,
        out_shape=tuple(outs),
        in_specs=[VMEM] * len(arrays),
        out_specs=(VMEM,) * len(outs),
        cost_estimate=pl.CostEstimate(flops=flops, bytes_accessed=moved, transcendentals=0),
        compiler_params=pltpu.CompilerParams(vmem_limit_bytes=24 << 20),
        name=kernel.__name__,
    )(*arrays)


def store_halves(keep_ref, send_ref, cols, value):
    half = keep_ref.shape[0]
    keep_ref[:, cols] = value[:half]
    send_ref[:, cols] = value[half:].astype(BF)


def forward_kernel(own, near, beside, wg, wu, wd, keep_ref, send_ref):
    rows = jnp.concatenate([own[...], near[...], beside[...]], axis=0)
    act, _ = silu_pair(jnp.dot(rows, wg[...], preferred_element_type=F32))
    hidden = (act * jnp.dot(rows, wu[...], preferred_element_type=F32)).astype(BF)
    for at in range(0, wd.shape[1], CHUNK):
        cols = slice(at, at + CHUNK)
        value = jnp.dot(hidden, wd[:, cols], preferred_element_type=F32)
        store_halves(keep_ref, send_ref, cols, value)


def saved(own, near, beside, width, units):
    pre = jnp.concatenate(
        [ref[:, width : width + 2 * units] for ref in (own, near, beside)], axis=0
    ).astype(F32)
    return pre[:, :units], pre[:, units:]


def grad_kernel(own, near, beside, out_ref):
    units, width = out_ref.shape
    gate, up = saved(own, near, beside, width, units)
    act, _ = silu_pair(gate)
    hidden = (act * up).astype(BF).T
    for at in range(0, width, CHUNK):
        cols = slice(at, at + CHUNK)
        rows = jnp.concatenate([own[:, cols], near[:, cols], beside[:, cols]], axis=0)
        out_ref[:, cols] = jnp.dot(hidden, rows, preferred_element_type=F32).astype(BF)


def backward_kernel(own, near, beside, wg, wu, wd, keep_ref, send_ref):
    units, width = wd.shape
    gate, up = saved(own, near, beside, width, units)
    act, slope = silu_pair(gate)
    rows = jnp.concatenate([own[:, :width], near[:, :width], beside[:, :width]], axis=0)
    dhid = lax.dot_general(rows, wd[...], CONTRACT, preferred_element_type=F32)
    d_gate = (dhid * up * slope).astype(BF)
    d_up = (dhid * act).astype(BF)
    for at in range(0, width, CHUNK):
        cols = slice(at, at + CHUNK)
        value = lax.dot_general(d_gate, wg[cols, :], CONTRACT, preferred_element_type=F32)
        value += lax.dot_general(d_up, wu[cols, :], CONTRACT, preferred_element_type=F32)
        store_halves(keep_ref, send_ref, cols, value)


def pair_kernel(keep_ref, got_ref, own_ref, send_ref):
    half = own_ref.shape[0]
    for at in range(0, keep_ref.shape[1], CHUNK):
        cols = slice(at, at + CHUNK)
        store_halves(own_ref, send_ref, cols, keep_ref[:, cols] + got_ref[:, cols].astype(F32))


def halves_of(rows, width):
    half = rows // 2
    return [jax.ShapeDtypeStruct((half, width), F32), jax.ShapeDtypeStruct((half, width), BF)]


def reduce_shards(keep, send):
    rows, width = keep.shape
    own, send = call(pair_kernel, halves_of(rows, width), rows * width, keep, swap(send, 1))
    return (own + swap(send, 2).astype(F32)).astype(BF)


def combine(table, rows):
    return lax.dot_general(
        table,
        rows.astype(F32),
        (((0,), (0,)), ((), ())),
        precision=lax.Precision.HIGHEST,
        preferred_element_type=F32,
    ).astype(BF)


def on_device(x_fwd, ids_fwd, prob_fwd, grad_bwd, ids_bwd, prob_bwd, pre_bwd, w_gate, w_up, w_down):
    tokens, width = x_fwd.shape[1:]
    wg, wu, wd = w_gate[0], w_up[0], w_down[0]
    units = wg.shape[1]
    index = lax.axis_index("expert")
    place = jnp.stack([index % SHARDS, far_half(index // SHARDS)]).astype(jnp.int32)
    send, table_f, table_b = build_rows(
        place, ids_fwd[0].T, prob_fwd[0].T, x_fwd[0], ids_bwd[0].T, prob_bwd[0].T, grad_bwd[0],
        pre_bwd[0].reshape(tokens, -1),
    )
    sections = lax.axis_size("pipe")
    onward = [(i, (i + 1) % sections) for i in range(sections)]
    table_f = lax.ppermute(table_f, "pipe", onward)

    got = route(send.reshape(EXPERTS, SLOTS, -1)).reshape(ROWS, -1)
    pair, near, far, end = width + 2 * units, width + 4 * units, width + 6 * units, width + 8 * units
    other_g = swap(jnp.concatenate([got[:, :width], got[:, near:end]], axis=1), 2)
    got_x = got[:, end:]
    other_x = swap(got_x, 2)

    own_g = got[:, :near]
    mine = jnp.concatenate([own_g, other_g], axis=0)
    beside = swap(jnp.concatenate([mine[:, :width], mine[:, pair:]], axis=1), 1)
    work = 2 * SHARDS * ROWS * width * units
    (partial,) = call(
        grad_kernel, [jax.ShapeDtypeStruct(wd.shape, BF)], work, own_g, other_g, beside
    )
    grad_rows = lax.psum_scatter(partial, "dp", scatter_dimension=0, tiled=True).astype(F32)

    outs = halves_of(SHARDS * ROWS, width)
    beside_x = swap(jnp.concatenate([got_x, other_x], axis=0), 1)
    keep_y, send_y = call(
        forward_kernel, outs, 3 * work, got_x, other_x, beside_x, wg, wu, wd
    )
    keep_dx, send_dx = call(
        backward_kernel, outs, 3 * work, own_g, other_g, beside, wg, wu, wd
    )
    part_y = lax.ppermute(reduce_shards(keep_y, send_y), "pipe", onward)
    part_dx = reduce_shards(keep_dx, send_dx)

    back = jnp.concatenate([part_y, part_dx], axis=1).reshape(EXPERTS, SLOTS, -1)
    back = route(back).reshape(ROWS, -1)
    routed = combine(table_f, back[:, :width])
    grad_input = combine(table_b, back[:, width:])
    return (routed[None], grad_input[None], grad_rows[None])


def solution(mesh):
    token = P("pipe", ("expert", "dp"), None)
    in_specs = (
        token, token, token, token, token, token,
        P("pipe", ("expert", "dp"), None, None, None),
        P("pipe", None, "expert"),
        P("pipe", None, "expert"),
        P("pipe", "expert", None),
    )
    return jax.shard_map(
        on_device, mesh=mesh, in_specs=in_specs, out_specs=(token, token, token), check_vma=False
    )
```

```python
import functools

import jax
import jax.numpy as jnp
from jax import lax
from jax.experimental import pallas as pl
from jax.experimental.pallas import tpu as pltpu
from jax.sharding import PartitionSpec as P

EXPERT = "expert"
EXPERTS = 16
SLOTS = 2
SHARDS = 4
ROWS = EXPERTS * SLOTS
CHUNK = 512
BF = jnp.bfloat16
F32 = jnp.float32


def route_groups(replicas):
    groups = []
    for r in range(replicas):
        for shard in range(SHARDS):
            groups.append(
                [
                    (e * SHARDS + (shard ^ 2 * far_half(e))) * replicas
                    + (r if e < EXPERTS // 2 else replicas - 1 - r)
                    for e in range(EXPERTS)
                ]
            )
    return groups


def far_half(expert):
    ring = EXPERTS // 2
    return expert % ring // (ring // 2)


def route(rows):
    groups = route_groups(lax.axis_size("dp"))
    return lax.all_to_all(
        rows,
        ("expert", "dp"),
        split_axis=0,
        concat_axis=0,
        tiled=True,
        axis_index_groups=groups,
    )


def swap(rows, bit):
    count = lax.axis_size("expert")
    return lax.ppermute(rows, "expert", [(i, i ^ bit) for i in range(count)])


def selections(ids_ref):
    chosen, tokens = ids_ref.shape
    row = lax.broadcasted_iota(jnp.int32, (ROWS, tokens), 0)
    hits = [ids_ref[k : k + 1, :] == row // SLOTS for k in range(chosen)]
    hit = jnp.where(functools.reduce(jnp.logical_or, hits), 1.0, 0.0)
    first = lax.broadcasted_iota(jnp.int32, (tokens, tokens), 0)
    second = lax.broadcasted_iota(jnp.int32, (tokens, tokens), 1)
    earlier = jnp.where(first < second, 1.0, 0.0)
    before = jnp.dot(hit, earlier, preferred_element_type=F32)
    slot = (row % SLOTS).astype(F32)
    return [jnp.where(jnp.logical_and(h, before == slot), 1.0, 0.0) for h in hits]


def pick(sel, rows):
    return jnp.dot(sel.astype(BF), rows, preferred_element_type=F32)


def build_kernel(*refs):
    hbm, (send_ref, wf_ref, tb_ref), held, sem = refs[:7], refs[7:10], refs[10:17], refs[17]
    copies = [
        pltpu.make_async_copy(src, dst, sem.at[i]) for i, (src, dst) in enumerate(zip(hbm, held))
    ]
    for copy in copies:
        copy.start()
    for copy in copies:
        copy.wait()
    ids_f, prob_f, x_ref, ids_b, prob_b, g_ref, pre_ref = held

    def store(at, rows):
        size = rows.shape[1]
        send_ref[:, :, at : at + size] = rows.reshape(EXPERTS, SLOTS, size).astype(BF)

    tokens, width = g_ref.shape
    sel_b = selections(ids_b)
    both = functools.reduce(jnp.add, sel_b)
    scaled = functools.reduce(jnp.add, [s * prob_b[k : k + 1, :] for k, s in enumerate(sel_b)])
    scale = jnp.sum(scaled, axis=1, keepdims=True)
    for at in range(0, width, CHUNK):
        store(at, scale * pick(both, g_ref[:, at : at + CHUNK]))
    chosen, hid = pre_ref.shape[1], pre_ref.shape[3]
    units = hid // SHARDS
    index = lax.axis_index(EXPERT)
    shard = index % SHARDS
    count = 2 * tokens * chosen
    column = lax.broadcasted_iota(jnp.int32, (tokens, count), 1)
    token = lax.broadcasted_iota(jnp.int32, (tokens, count), 0)
    rows = pre_ref[...].astype(F32).reshape(count, hid).astype(BF)
    halves = []
    for half in range(2):
        sel = jnp.zeros((ROWS, count), F32)
        for k, one in enumerate(sel_b):
            spread = jnp.where(column == (token * chosen + k) * 2 + half, 1.0, 0.0)
            sel += jnp.dot(one, spread, preferred_element_type=F32)
        halves.append(pick(sel, rows))
    blocks = [[h[:, s * units : (s + 1) * units] for h in halves] for s in range(SHARDS)]
    expert = lax.broadcasted_iota(jnp.int32, (ROWS, units), 0) // SLOTS
    crosses = far_half(expert) != far_half(index // SHARDS)
    target = jnp.where(crosses, shard ^ 2, shard)
    for step in range(SHARDS):
        for half in range(2):
            part = functools.reduce(
                jnp.add,
                [jnp.where((target ^ step) == s, blocks[s][half], 0.0) for s in range(SHARDS)],
            )
            store(width + (2 * step + half) * units, part)
    tb_ref[...] = both
    sel_f = selections(ids_f)
    both = functools.reduce(jnp.add, sel_f)
    for at in range(0, width, CHUNK):
        store(width + 2 * hid + at, pick(both, x_ref[:, at : at + CHUNK]))
    wf_ref[...] = functools.reduce(
        jnp.add, [s * prob_f[k : k + 1, :] for k, s in enumerate(sel_f)]
    )


VMEM = pl.BlockSpec(memory_space=pltpu.VMEM)
HBM = pl.BlockSpec(memory_space=pltpu.HBM)


def build_rows(*arrays):
    x, pre = arrays[2], arrays[6]
    tokens, width = x.shape
    total = 2 * width + 2 * pre.shape[3]
    return pl.pallas_call(
        build_kernel,
        out_shape=(
            jax.ShapeDtypeStruct((EXPERTS, SLOTS, total), BF),
            jax.ShapeDtypeStruct((ROWS, tokens), F32),
            jax.ShapeDtypeStruct((ROWS, tokens), F32),
        ),
        in_specs=[HBM] * len(arrays),
        out_specs=(VMEM,) * 3,
        scratch_shapes=[pltpu.VMEM(a.shape, a.dtype) for a in arrays]
        + [pltpu.SemaphoreType.DMA((len(arrays),))],
        cost_estimate=pl.CostEstimate(
            flops=4 * ROWS * tokens * width, bytes_accessed=2 << 20, transcendentals=0
        ),
        compiler_params=pltpu.CompilerParams(vmem_limit_bytes=56 << 20),
        name="build_rows",
    )(*arrays)


def silu_pair(value):
    sig = jax.nn.sigmoid(value)
    return (value * sig, sig * (1.0 + value * (1.0 - sig)))


CONTRACT = (((1,), (1,)), ((), ()))


def call(kernel, outs, flops, *arrays):
    moved = sum(a.size * a.dtype.itemsize for a in arrays)
    moved += sum(o.size * o.dtype.itemsize for o in outs)
    return pl.pallas_call(
        kernel,
        out_shape=tuple(outs),
        in_specs=[VMEM] * len(arrays),
        out_specs=(VMEM,) * len(outs),
        cost_estimate=pl.CostEstimate(flops=flops, bytes_accessed=moved, transcendentals=0),
        compiler_params=pltpu.CompilerParams(vmem_limit_bytes=24 << 20),
        name=kernel.__name__,
    )(*arrays)


def store_halves(keep_ref, send_ref, cols, value):
    half = keep_ref.shape[0]
    keep_ref[:, cols] = value[:half]
    send_ref[:, cols] = value[half:].astype(BF)


def forward_kernel(own, near, beside, wg, wu, wd, keep_ref, send_ref):
    rows = jnp.concatenate([own[...], near[...], beside[...]], axis=0)
    act, _ = silu_pair(jnp.dot(rows, wg[...], preferred_element_type=F32))
    hidden = (act * jnp.dot(rows, wu[...], preferred_element_type=F32)).astype(BF)
    for at in range(0, wd.shape[1], CHUNK):
        cols = slice(at, at + CHUNK)
        value = jnp.dot(hidden, wd[:, cols], preferred_element_type=F32)
        store_halves(keep_ref, send_ref, cols, value)


def saved(own, near, beside, width, units):
    pre = jnp.concatenate(
        [ref[:, width : width + 2 * units] for ref in (own, near, beside)], axis=0
    ).astype(F32)
    return pre[:, :units], pre[:, units:]


def grad_kernel(own, near, beside, out_ref):
    units, width = out_ref.shape
    gate, up = saved(own, near, beside, width, units)
    act, _ = silu_pair(gate)
    hidden = (act * up).astype(BF).T
    for at in range(0, width, CHUNK):
        cols = slice(at, at + CHUNK)
        rows = jnp.concatenate([own[:, cols], near[:, cols], beside[:, cols]], axis=0)
        out_ref[:, cols] = jnp.dot(hidden, rows, preferred_element_type=F32).astype(BF)


def backward_kernel(own, near, beside, wg, wu, wd, keep_ref, send_ref):
    units, width = wd.shape
    gate, up = saved(own, near, beside, width, units)
    act, slope = silu_pair(gate)
    rows = jnp.concatenate([own[:, :width], near[:, :width], beside[:, :width]], axis=0)
    dhid = lax.dot_general(rows, wd[...], CONTRACT, preferred_element_type=F32)
    d_gate = (dhid * up * slope).astype(BF)
    d_up = (dhid * act).astype(BF)
    for at in range(0, width, CHUNK):
        cols = slice(at, at + CHUNK)
        value = lax.dot_general(d_gate, wg[cols, :], CONTRACT, preferred_element_type=F32)
        value += lax.dot_general(d_up, wu[cols, :], CONTRACT, preferred_element_type=F32)
        store_halves(keep_ref, send_ref, cols, value)


def pair_kernel(keep_ref, got_ref, own_ref, send_ref):
    half = own_ref.shape[0]
    for at in range(0, keep_ref.shape[1], CHUNK):
        cols = slice(at, at + CHUNK)
        store_halves(own_ref, send_ref, cols, keep_ref[:, cols] + got_ref[:, cols].astype(F32))


def halves_of(rows, width):
    half = rows // 2
    return [jax.ShapeDtypeStruct((half, width), F32), jax.ShapeDtypeStruct((half, width), BF)]


def reduce_shards(keep, send):
    rows, width = keep.shape
    own, send = call(pair_kernel, halves_of(rows, width), rows * width, keep, swap(send, 1))
    return (own + swap(send, 2).astype(F32)).astype(BF)


def combine(table, rows):
    return lax.dot_general(
        table,
        rows.astype(F32),
        (((0,), (0,)), ((), ())),
        precision=lax.Precision.HIGHEST,
        preferred_element_type=F32,
    ).astype(BF)


def on_device(x_fwd, ids_fwd, prob_fwd, grad_bwd, ids_bwd, prob_bwd, pre_bwd, w_gate, w_up, w_down):
    tokens, width = x_fwd.shape[1:]
    wg, wu, wd = w_gate[0], w_up[0], w_down[0]
    units = wg.shape[1]
    send, table_f, table_b = build_rows(
        ids_fwd[0].T, prob_fwd[0].T, x_fwd[0], ids_bwd[0].T, prob_bwd[0].T, grad_bwd[0],
        pre_bwd[0],
    )
    sections = lax.axis_size("pipe")
    onward = [(i, (i + 1) % sections) for i in range(sections)]
    table_f = lax.ppermute(table_f, "pipe", onward)

    got = route(send).reshape(ROWS, -1)
    pair, near, far, end = width + 2 * units, width + 4 * units, width + 6 * units, width + 8 * units
    other_g = swap(jnp.concatenate([got[:, :width], got[:, near:end]], axis=1), 2)
    got_x = got[:, end:]
    other_x = swap(got_x, 2)

    own_g = got[:, :near]
    mine = jnp.concatenate([own_g, other_g], axis=0)
    beside = swap(jnp.concatenate([mine[:, :width], mine[:, pair:]], axis=1), 1)
    work = 2 * SHARDS * ROWS * width * units
    (partial,) = call(
        grad_kernel, [jax.ShapeDtypeStruct(wd.shape, BF)], work, own_g, other_g, beside
    )
    grad_rows = lax.psum_scatter(partial, "dp", scatter_dimension=0, tiled=True).astype(F32)

    outs = halves_of(SHARDS * ROWS, width)
    beside_x = swap(jnp.concatenate([got_x, other_x], axis=0), 1)
    keep_y, send_y = call(
        forward_kernel, outs, 3 * work, got_x, other_x, beside_x, wg, wu, wd
    )
    keep_dx, send_dx = call(
        backward_kernel, outs, 3 * work, own_g, other_g, beside, wg, wu, wd
    )
    part_y = lax.ppermute(reduce_shards(keep_y, send_y), "pipe", onward)
    part_dx = reduce_shards(keep_dx, send_dx)

    back = jnp.concatenate([part_y, part_dx], axis=1).reshape(EXPERTS, SLOTS, -1)
    back = route(back).reshape(ROWS, -1)
    routed = combine(table_f, back[:, :width])
    grad_input = combine(table_b, back[:, width:])
    return (routed[None], grad_input[None], grad_rows[None])


def solution(mesh):
    token = P("pipe", ("expert", "dp"), None)
    in_specs = (
        token, token, token, token, token, token,
        P("pipe", ("expert", "dp"), None, None, None),
        P("pipe", None, "expert"),
        P("pipe", None, "expert"),
        P("pipe", "expert", None),
    )
    return jax.shard_map(
        on_device, mesh=mesh, in_specs=in_specs, out_specs=(token, token, token), check_vma=False
    )
```
